32 devices in a mesh: bucket: 8 (over z, core), replica: 4 (over y, x).
Axes of the slice: x: 2, y: 2, z: 4, core: 2. Of those that a mesh axis runs over, the one named last changes fastest.
Arguments:
- rows: bfloat16 [32768, 768], P(('bucket', 'replica')), may hold values from -40 to 40, as said below
- cell_ids: int32 [32768, 1], P(('bucket', 'replica')), may hold values from 0 to 15; in each aligned block of 1024 rows (0 to 1023, 1024 to 2047, ...) at most 128 rows name the same one
- start_basis: float32 [16, 768, 768], P('bucket'), may hold values from -0.1 to 1.1, as said below
Outputs:
- rotated: bfloat16 [32768, 768], P(('bucket', 'replica'))
The draws below stay inside these ranges and needn't reach their ends.
Inputs may be any that keep to these rules, and one draw needn't show every extreme that they name: `cell_ids`: in the rows of one device no cell is named by more than 128 rows, a bound that some block reaches; every cell is named by some row. `rows`: A residual row: a column offset plus rough noise with column and row scales. `start_basis`: the identity plus small dense entries.
All inputs are finite; a program needn't handle non-finite values.
Results may differ from the reference program's by a relative error of at most 0.0049.
Values may be sent and summed in bfloat16 or wider, within the bound.
No kernel may reach another device: no remote copies, remote signals or barrier semaphores. Data moves between devices by JAX's collectives and lax.ppermute only.
A program may use at most 128 MiB of HBM per device.

```python
import math
import jax
import jax.numpy as jnp
import numpy as np
from jax import lax

D = 768
CELLS = 16
ROWS_DEV = 1024
ITERS_NS = 3
CAP = 128
ROWS = 32768


def draw_rows(key, part):
    keys = jax.random.split(key, 4)
    column_scale = jnp.exp(jax.random.uniform(keys[0], (1, D), jnp.float32, 0.0, math.log(4.0)))
    offset = jax.random.uniform(keys[1], (1, D), jnp.float32, -1.0, 1.0)
    row_scale = jnp.exp(jax.random.uniform(keys[2], (ROWS, 1), jnp.float32, math.log(0.3), math.log(3.0)))
    noise = jax.random.normal(keys[3], (ROWS, D), jnp.float32)
    values = jnp.clip(offset + noise * column_scale * row_scale, -40.0, 40.0)
    return values.astype(jnp.bfloat16)


def draw_start_basis(key, part):
    noise = jnp.clip(jax.random.normal(key, (CELLS, D, D), jnp.float32) * (0.5 / math.sqrt(D)), -0.1, 0.1)
    return jnp.eye(D, dtype=jnp.float32)[None, :, :] + noise


def assign_block(rng, own, number, rows, amount, top, bound, skew):
    order = jax.random.permutation(rng, amount)
    crowded, common = shares(amount, rows * top, bound, skew, True), shares(amount, rows * top, bound, skew, False)
    places = jnp.arange(amount)

    def named(lengths, offset_by):
        used = int((lengths > 0).sum())
        fixed = max(1, used // 4)
        shifted = fixed + (places - fixed + offset_by * (used - fixed)) % max(1, amount - fixed)
        return jnp.zeros((amount,), jnp.int32).at[order[jnp.where(places < fixed, places, shifted)]].set(jnp.asarray(lengths, jnp.int32))

    lengths = jnp.where(number % 4 == 0, named(crowded, number // 4), named(common, number - number // 4 - 1))
    mixed = jax.random.permutation(jax.random.fold_in(own, 3), amount)
    source_of, receiver = mixed[0:amount // 2 * 2:2], mixed[1:amount // 2 * 2:2]
    slack = jnp.minimum(lengths[source_of] - 1, bound - lengths[receiver]) // 2
    slack = jnp.where((source_of == order[0]) | (receiver == order[0]) | (lengths[receiver] == 0), 0, jnp.maximum(slack, 0))
    shifted = jax.random.randint(jax.random.fold_in(own, 4), (amount // 2,), 0, 1 << 20) % (slack + 1)
    lengths = lengths.at[source_of].add(-shifted).at[receiver].add(shifted)
    labels = jnp.searchsorted(jnp.cumsum(lengths), jnp.arange(rows * top), side="right").astype(jnp.int32)
    listing = labels.reshape(top, rows).T
    listing = listing[jax.random.permutation(jax.random.fold_in(own, 1), rows)]
    offset_by = jax.random.randint(jax.random.fold_in(own, 2), (rows, 1), 0, top)
    return jnp.take_along_axis(listing, (jnp.arange(top)[None, :] + offset_by) % top, axis=1)


def shares(number_of, total, limit, slope, full):
    portions = [(1 << 20) // math.isqrt(standing ** slope) + 1 for standing in range(1, number_of + 1)]
    largest = limit if full else min(limit, max(-(-total // number_of), total * portions[0] // sum(portions)))
    least = 1 if total - largest >= number_of - 1 else 0
    given, rest = [largest] + [least] * (number_of - 1), total - largest - least * (number_of - 1)
    while rest > 0:
        movable = [i for i in range(1, number_of) if given[i] < largest] or [i for i in range(1, number_of) if given[i] < limit]
        whole, budget = sum([portions[i] for i in movable]), rest
        for i in movable:
            extra = min(limit - given[i], max(1, budget * portions[i] // whole), rest)
            given[i] = given[i] + extra
            rest = rest - extra
    return np.array(given)


def setup_inputs(seed: int = 0) -> dict:
    arg_keys = jax.random.split(jax.random.key(seed), 4)
    rows = draw_rows(jax.random.fold_in(arg_keys[3], 71), 0)
    cell_ids_keys = jax.random.split(jax.random.fold_in(arg_keys[1], 1), ROWS // ROWS_DEV)
    cell_ids_turns = jax.random.permutation(jax.random.fold_in(arg_keys[1], 3), ROWS // ROWS_DEV)
    cell_ids = jax.vmap(lambda own, number: assign_block(jax.random.fold_in(arg_keys[1], 2), own, number, ROWS_DEV, CELLS, 1, CAP, 0))(cell_ids_keys, cell_ids_turns).reshape((ROWS, 1))
    start_basis = draw_start_basis(jax.random.fold_in(arg_keys[3], 71), 0)
    return dict(rows=rows, cell_ids=cell_ids, start_basis=start_basis)


def orthogonalise(count, total, square, basis):
    mean = total / jnp.maximum(count, 1.0)
    covariance = square / jnp.maximum(count, 1.0) - mean[:, None] * mean[None, :]
    current = basis
    for step in range(ITERS_NS):
        image = jnp.dot(covariance, current, precision=lax.Precision.HIGHEST)
        gram_matrix = jnp.dot(image.T, image, precision=lax.Precision.HIGHEST)
        factor = jnp.linalg.cholesky(gram_matrix)
        current = jax.scipy.linalg.solve_triangular(factor, image.T, lower=True).T
    rotation = current.astype(jnp.bfloat16)
    shift = jnp.dot(mean, rotation.astype(jnp.float32), precision=lax.Precision.HIGHEST)
    return (rotation, shift)

def reference(rows, cell_ids, start_basis):
    total_rows = rows.shape[0]
    width = rows.shape[1]
    flat_ids = cell_ids[:, 0].astype(jnp.int32)
    order = jnp.argsort(flat_ids, stable=True).astype(jnp.int32)
    onehot = (flat_ids[:, None] == jnp.arange(CELLS, dtype=jnp.int32)[None, :]).astype(jnp.int32)
    counts = jnp.sum(onehot, axis=0).astype(jnp.int32)
    starts = (jnp.cumsum(counts) - counts).astype(jnp.int32)
    block = 1024
    sorted_rows = jnp.concatenate([rows[order], jnp.zeros((block, width), rows.dtype)], axis=0)
    positions = jnp.arange(block, dtype=jnp.int32)

    def block_range(cell):
        first = starts[cell]
        last = first + counts[cell]
        return (first, last, (first // block).astype(jnp.int32), ((last + block - 1) // block).astype(jnp.int32))

    def moments(cell):
        first, last, lower, upper = block_range(cell)

        def add_block(index, carry):
            total, square = carry
            begin = (index * block).astype(jnp.int32)
            piece = lax.dynamic_slice_in_dim(sorted_rows, begin, block, 0)
            keep = (begin + positions >= first) & (begin + positions < last)
            piece = jnp.where(keep[:, None], piece, jnp.zeros_like(piece))
            total = total + jnp.sum(piece, axis=0, dtype=jnp.float32)
            square = square + jnp.dot(piece.T.astype(jnp.float32), piece.astype(jnp.float32), preferred_element_type=jnp.float32)
            return (total, square)
        start_carry = (jnp.zeros((width,), jnp.float32), jnp.zeros((width, width), jnp.float32))
        return lax.fori_loop(lower, upper, add_block, start_carry)
    totals, squares = lax.map(moments, jnp.arange(CELLS, dtype=jnp.int32))

    def one_cell(packed):
        return orthogonalise(packed[0], packed[1], packed[2], packed[3])
    rotations, shifts = lax.map(one_cell, (counts.astype(jnp.float32), totals, squares, start_basis))

    def rotate_cell(cell, sorted_out):
        first, last, lower, upper = block_range(cell)
        rotation = rotations[cell]
        shift = shifts[cell]

        def write_block(index, buffer):
            begin = (index * block).astype(jnp.int32)
            piece = lax.dynamic_slice_in_dim(sorted_rows, begin, block, 0)
            value = (jnp.dot(piece.astype(jnp.float32), rotation.astype(jnp.float32), preferred_element_type=jnp.float32) - shift[None, :]).astype(jnp.bfloat16)
            keep = (begin + positions >= first) & (begin + positions < last)
            previous = lax.dynamic_slice_in_dim(buffer, begin, block, 0)
            return lax.dynamic_update_slice_in_dim(buffer, jnp.where(keep[:, None], value, previous), begin, 0)
        return lax.fori_loop(lower, upper, write_block, sorted_out)
    sorted_out = lax.fori_loop(0, CELLS, rotate_cell, jnp.zeros((total_rows + block, width), jnp.bfloat16))
    return jnp.zeros((total_rows, width), jnp.bfloat16).at[order].set(sorted_out[:total_rows])
```

```python
import functools
import jax
import jax.numpy as jnp
from jax import lax
from jax.experimental import pallas as pl
from jax.experimental.pallas import tpu as pltpu
from jax.sharding import Mesh, PartitionSpec as P

CELLS = 16
ITERS_NS = 3
CAP = 128
BLK = 128
SUB = 16
WIDE = 256
PAD_MARK = 128.0
F32 = jnp.float32
BF16 = jnp.bfloat16
NT = (((1,), (1,)), ((), ()))
VMEM_LIMIT = 56 * 1024 * 1024


def split(value):
    high = value.astype(BF16)
    return high, (value - high.astype(F32)).astype(BF16)


def dot(left, right):
    return jnp.dot(left, right, preferred_element_type=F32)


def dot_nt(left, right):
    return lax.dot_general(left, right, NT, preferred_element_type=F32)


def product(left, right, multiply=dot):
    high, low = left
    size = high.shape[0]
    both = multiply(jnp.concatenate([high, low], axis=0), right[0])
    return both[:size, :] + (both[size:, :] + multiply(high, right[1]))


def inverse_factors(squares):
    steps = BLK // SUB
    chains = range(len(squares))
    lane = lax.broadcasted_iota(jnp.int32, (SUB, BLK), 1)
    line = lax.broadcasted_iota(jnp.int32, (SUB, BLK), 0)
    even = lax.broadcasted_iota(jnp.int32, (SUB, 2 * BLK), 0) % 2 == 0
    parts = [[square[SUB * b : SUB * (b + 1), :] for b in range(steps)] for square in squares]
    units = [[(lane == line + SUB * b).astype(F32) for b in range(steps)] for _ in chains]
    done = [[] for _ in chains]

    def begin(n, b):
        row, carry = parts[n][b], units[n][b]
        first = SUB * b
        column = [
            jnp.broadcast_to(row[:, first + k : first + k + 1], (SUB, BLK)) for k in range(SUB)
        ]
        zeros = jnp.zeros((SUB, BLK), F32)
        return dict(
            column=column, row=row, carry=carry, forward=carry, pivots=zeros, alpha=zeros, beta=zeros
        )

    def advance(state, k):
        q = k + 1
        column = state["column"]
        one, two = column[k], column[q]
        head, side = one[k : k + 1, :], one[q : q + 1, :]
        cross, tail = two[k : k + 1, :], two[q : q + 1, :]
        det = head * tail - cross * side
        inverse = 1.0 / det
        pair = (line == k) | (line == q)
        ratio_one = jnp.where(pair, 0.0, one * tail - two * side) * inverse
        ratio_two = jnp.where(pair, 0.0, two * head - one * cross) * inverse

        def clear(value, left, right):
            return value - (left * value[k : k + 1, :] + right * value[q : q + 1, :])

        for j in range(k + 2, SUB):
            column[j] = clear(column[j], ratio_one, ratio_two)
        state["row"] = clear(state["row"], ratio_one, ratio_two)
        state["carry"] = clear(state["carry"], ratio_one, ratio_two)
        single = 1.0 / head
        low_one = jnp.where(line > q, ratio_one, jnp.where(line == q, side * single, 0.0))
        low_two = jnp.where(line > q, ratio_two, 0.0)
        state["forward"] = clear(state["forward"], low_one, low_two)

        def keep(name, upper, lower):
            state[name] = jnp.where(line == k, upper, jnp.where(line == q, lower, state[name]))

        keep("pivots", head, det * single)
        keep("alpha", tail * inverse, head * inverse)
        keep("beta", -cross * inverse, -side * inverse)

    def finish(n, b, state):
        done[n].append(state["forward"] * lax.rsqrt(state["pivots"]))
        if b + 1 == steps:
            return
        part, unit = parts[n], units[n]
        rest = jnp.concatenate(part[b + 1 :], axis=0)
        place = (lax.broadcasted_iota(jnp.int32, rest.shape, 1) - SUB * b) % BLK // SUB
        high = rest.astype(BF16).astype(F32)
        low = rest - high
        terms = jnp.where(place == 0, high, 0.0)
        terms = jnp.where(place == 1, pltpu.roll(low, SUB, 1), terms)
        terms = jnp.where(place == 2, pltpu.roll(high, 2 * SUB, 1), terms).astype(BF16)
        both = jnp.concatenate([state["row"], state["carry"]], axis=1)
        swapped = jnp.where(even, pltpu.roll(both, SUB - 1, 0), pltpu.roll(both, 1, 0))
        alpha = jnp.concatenate([state["alpha"]] * 2, axis=1)
        beta = jnp.concatenate([state["beta"]] * 2, axis=1)
        both_high, both_low = split(alpha * both + beta * swapped)
        filled = [jnp.zeros((SUB, 2 * BLK), BF16)] * steps
        filled[b] = both_high
        filled[(b + 1) % steps] = both_high
        filled[(b + 2) % steps] = both_low
        update = dot(terms, jnp.concatenate(filled, axis=0))
        for i in range(b + 1, steps):
            at = SUB * (i - b - 1)
            part[i] = part[i] - update[at : at + SUB, :BLK]
            unit[i] = unit[i] - update[at : at + SUB, BLK:]

    for b in range(steps):
        states = [begin(n, b) for n in chains]
        for k in range(0, SUB, 2):
            for state in states:
                advance(state, k)
        for n in chains:
            finish(n, b, states[n])
    return [jnp.concatenate(pieces, axis=0) for pieces in done]


def inverse_factors_wide(squares):
    firsts = inverse_factors([square[:BLK, :BLK] for square in squares])
    terms = [split(first) for first in firsts]
    factors = [
        split(product(split(square[BLK:, :BLK]), term, dot_nt))
        for square, term in zip(squares, terms)
    ]
    seconds = inverse_factors(
        [
            square[BLK:, BLK:] - product(factor, factor, dot_nt)
            for square, factor in zip(squares, factors)
        ]
    )
    results = []
    for first, term, factor, second in zip(firsts, terms, factors, seconds):
        corner = product(split(second), split(product(factor, term)))
        upper = jnp.concatenate([first, jnp.zeros((BLK, BLK), F32)], axis=1)
        results.append(
            jnp.concatenate([upper, jnp.concatenate([-corner, second], axis=1)], axis=0)
        )
    return results


FIRST, SECOND = slice(0, WIDE), slice(WIDE, 2 * WIDE)


def terms_of(ref):
    return ref[FIRST, :], ref[SECOND, :]


def wave(cov_ref, tasks):
    width = cov_ref.shape[1]
    images, grams = [], []
    for source, before_refs, _ in tasks:
        image = product(source, (cov_ref[:width, :], cov_ref[width:, :]))
        if before_refs:
            image_terms = split(image)
            for before_ref in before_refs:
                before = terms_of(before_ref)
                along = split(product(image_terms, before, dot_nt))
                image = image - product(along, before)
        image_terms = split(image)
        images.append(image_terms)
        grams.append(product(image_terms, image_terms, dot_nt))
    for inverse, image_terms, task in zip(inverse_factors_wide(grams), images, tasks):
        high, low = split(product(split(inverse), image_terms))
        task[2][FIRST, :] = high
        task[2][SECOND, :] = low


def rotate(mean, rows_ref, rotation, out_ref, columns):
    width = mean.shape[1]
    high = mean.astype(BF16)
    left = mean - high.astype(F32)
    middle = left.astype(BF16)
    low = (left - middle.astype(F32)).astype(BF16)
    pieces = jnp.concatenate([high, middle, low, jnp.zeros((13, width), BF16)], axis=0)
    shift = jnp.sum(dot_nt(pieces, rotation), axis=0, keepdims=True)
    some = 512
    for n in range(rows_ref.shape[0] // some):
        at = slice(some * n, some * (n + 1))
        out_ref[at, columns] = (dot_nt(rows_ref[at, :], rotation) - shift).astype(BF16)


def first_kernel(
    moments_ref, moments_other_ref, start_ref, rows_hbm_ref,
    out_ref, cov_ref, mean_ref, q20_ref, q30_ref, q21_ref, q12_ref,
    rows_ref, q10_ref, q11_ref, sem,
):
    copy = pltpu.make_async_copy(rows_hbm_ref, rows_ref, sem)
    copy.start()
    width = cov_ref.shape[1]
    tail = moments_ref[width : width + 8, :] + moments_other_ref[width : width + 8, :]
    divisor = jnp.maximum(tail[1:2, :], 1.0)
    mean = tail[0:1, :] / divisor
    mean_rows = jnp.broadcast_to(mean, (BLK, width))
    for i in range(width // BLK):
        at = slice(BLK * i, BLK * (i + 1))
        mean_column = jnp.broadcast_to(mean_rows[:, at].T[:, :1], (BLK, width))
        square = moments_ref[at, :] + moments_other_ref[at, :]
        high, low = split(square / divisor - mean_column * mean)
        cov_ref[BLK * i : BLK * (i + 1), :] = high
        cov_ref[width + BLK * i : width + BLK * (i + 1), :] = low
    mean_ref[...] = jnp.broadcast_to(mean, mean_ref.shape)

    def start(i):
        return split(start_ref[WIDE * i : WIDE * (i + 1), :])

    wave(cov_ref, [(start(0), [], q10_ref)])
    wave(cov_ref, [(terms_of(q10_ref), [], q20_ref), (start(1), [q10_ref], q11_ref)])
    wave(
        cov_ref,
        [
            (terms_of(q20_ref), [], q30_ref),
            (terms_of(q11_ref), [q20_ref], q21_ref),
            (start(2), [q10_ref, q11_ref], q12_ref),
        ],
    )
    copy.wait()
    rotate(mean, rows_ref, q30_ref[FIRST, :], out_ref, FIRST)


def last_kernel(
    cov_ref, mean_ref, q20_ref, q30_ref, q21_ref, q12_ref, rows_hbm_ref,
    out_ref, rows_ref, q31_ref, q22_ref, q32_ref, sem,
):
    copy = pltpu.make_async_copy(rows_hbm_ref, rows_ref, sem)
    copy.start()
    mean = mean_ref[0:1, :]
    wave(
        cov_ref,
        [
            (terms_of(q21_ref), [q30_ref], q31_ref),
            (terms_of(q12_ref), [q20_ref, q21_ref], q22_ref),
        ],
    )
    copy.wait()
    rotate(mean, rows_ref, q31_ref[FIRST, :], out_ref, FIRST)
    wave(cov_ref, [(terms_of(q22_ref), [q30_ref, q31_ref], q32_ref)])
    rotate(mean, rows_ref, q32_ref[FIRST, :], out_ref, SECOND)


def in_vmem(amount):
    return [pl.BlockSpec(memory_space=pltpu.VMEM)] * amount


def stage(kernel, inputs, rows, outputs, kept, flops, name):
    amount, width = rows.shape
    terms = pltpu.VMEM((2 * WIDE, width), BF16)
    return pl.pallas_call(
        kernel,
        out_shape=outputs,
        in_specs=in_vmem(len(inputs)) + [pl.BlockSpec(memory_space=pl.ANY)],
        out_specs=in_vmem(len(outputs)),
        scratch_shapes=[pltpu.VMEM((amount, width), BF16)]
        + [terms] * kept
        + [pltpu.SemaphoreType.DMA(())],
        compiler_params=pltpu.CompilerParams(vmem_limit_bytes=VMEM_LIMIT),
        cost_estimate=pl.CostEstimate(
            flops=flops * width**3, bytes_accessed=20 * width * width, transcendentals=0
        ),
        name=name,
    )(*inputs, rows)


def moments_kernel(rows_ref, out_ref, kept_ref):
    amount, width = rows_ref.shape
    step = 256
    total = jnp.zeros((8, width), F32)
    count = jnp.zeros((8, 1), F32)
    for i in range(amount // step):
        at = slice(step * i, step * (i + 1))
        piece = rows_ref[at, :].astype(F32)
        valid = piece[:, :1] < PAD_MARK
        piece = jnp.where(valid, piece, 0.0)
        kept_ref[at, :] = piece.astype(BF16)
        total = total + jnp.sum(piece.reshape(step // 8, 8, width), axis=0)
        count = count + jnp.sum(valid.astype(F32).reshape(step // 8, 8, 1), axis=0)
    for n in range(width // 256):
        at = slice(256 * n, 256 * (n + 1))
        out_ref[at, :] = lax.dot_general(
            kept_ref[:, at], kept_ref[...], (((0,), (0,)), ((), ())), preferred_element_type=F32
        )
    line = lax.broadcasted_iota(jnp.int32, (8, width), 0)
    total = jnp.sum(total, axis=0, keepdims=True)
    count = jnp.sum(count, axis=0, keepdims=True)
    out_ref[width : width + 8, :] = jnp.where(line == 0, total, jnp.where(line == 1, count, 0.0))


def moments_of(rows):
    amount, width = rows.shape
    return pl.pallas_call(
        moments_kernel,
        out_shape=jax.ShapeDtypeStruct((width + 8, width), F32),
        in_specs=in_vmem(1),
        out_specs=pl.BlockSpec(memory_space=pltpu.VMEM),
        scratch_shapes=[pltpu.VMEM((amount, width), BF16)],
        compiler_params=pltpu.CompilerParams(vmem_limit_bytes=VMEM_LIMIT),
        name="moments",
    )(rows)


def pack_kernel(ids_ref, rows_ref, buffer_ref, place_ref):
    amount = ids_ref.shape[1]
    cell = lax.broadcasted_iota(jnp.int32, (CELLS, amount), 0)
    named = ids_ref[...] == cell
    upto = lax.broadcasted_iota(jnp.int32, (BLK, BLK), 0) <= lax.broadcasted_iota(
        jnp.int32, (BLK, BLK), 1
    )
    upto = upto.astype(BF16)
    onehot = named.astype(BF16)
    before = jnp.zeros((CELLS, 1), F32)
    goals = []
    for i in range(amount // BLK):
        at = slice(BLK * i, BLK * (i + 1))
        running = dot(onehot[:, at], upto) + before
        before = running[:, BLK - 1 :]
        goal = running - 1.0 + CAP * cell[:, at].astype(F32)
        goals.append(jnp.sum(jnp.where(named[:, at], goal, 0.0), axis=0, keepdims=True))
    goal = jnp.concatenate(goals, axis=1)
    for i in range(amount // BLK):
        at = slice(BLK * i, BLK * (i + 1))
        place_ref[at, :] = jnp.broadcast_to(goals[i], (BLK, BLK)).T
    group = 4
    slot = lax.broadcasted_iota(jnp.int32, (group * CAP, amount), 0).astype(F32)
    within = lax.broadcasted_iota(jnp.int32, (CAP, rows_ref.shape[1]), 0).astype(F32)
    for c in range(0, CELLS, group):
        hit = jnp.where(goal - float(CAP * c) == slot, 1.0, 0.0).astype(BF16)
        moved = dot(hit, rows_ref[...])
        for k in range(group):
            used = within < before[c + k : c + k + 1, :]
            part = jnp.where(used, moved[CAP * k : CAP * (k + 1), :], PAD_MARK)
            buffer_ref[c + k] = part.astype(BF16)


def unpack_kernel(place_ref, slots_ref, *refs):
    out_ref = refs[-1]
    amount, width = slots_ref.shape
    ahead = out_ref.shape[1] - width
    step = 256
    lane = lax.broadcasted_iota(jnp.int32, (step, amount), 1).astype(F32)
    for i in range(out_ref.shape[0] // step):
        at = slice(step * i, step * (i + 1))
        goal = jnp.broadcast_to(place_ref[at, :1], (step, amount))
        onehot = jnp.where(goal == lane, 1.0, 0.0).astype(BF16)
        out_ref[at, ahead:] = dot(onehot, slots_ref[...]).astype(BF16)
    first = 0
    for ready_ref in refs[:-1]:
        out_ref[:, first : first + ready_ref.shape[1]] = ready_ref[...]
        first += ready_ref.shape[1]


def pack(ids, rows):
    amount, width = rows.shape
    return pl.pallas_call(
        pack_kernel,
        out_shape=(
            jax.ShapeDtypeStruct((CELLS, CAP, width), BF16),
            jax.ShapeDtypeStruct((amount, BLK), F32),
        ),
        in_specs=in_vmem(2),
        out_specs=in_vmem(2),
        compiler_params=pltpu.CompilerParams(vmem_limit_bytes=VMEM_LIMIT),
        name="pack",
    )(ids, rows)


def unpack(place, slots, *ahead):
    width = slots.shape[1] + sum(piece.shape[1] for piece in ahead)
    return pl.pallas_call(
        unpack_kernel,
        out_shape=jax.ShapeDtypeStruct((place.shape[0], width), BF16),
        in_specs=in_vmem(2 + len(ahead)),
        out_specs=pl.BlockSpec(memory_space=pltpu.VMEM),
        compiler_params=pltpu.CompilerParams(vmem_limit_bytes=VMEM_LIMIT),
        cost_estimate=pl.CostEstimate(
            flops=2 * place.shape[0] * slots.size, bytes_accessed=4 * slots.size, transcendentals=0
        ),
        name="unpack",
    )(place, slots, *ahead)


def exchange(slots):
    width = slots.shape[-1]
    blocks = slots.reshape(CELLS, CAP, width)
    blocks = lax.all_to_all(blocks, ("z", "sub"), split_axis=0, concat_axis=0, tiled=True)
    return blocks.reshape(CELLS * CAP, width)


def body(owned, groups, rows, cell_ids, start_basis):
    width = rows.shape[1]
    swap = [(0, 1), (1, 0)]
    sub = lax.axis_index("sub")
    start = lax.dynamic_index_in_dim(start_basis, sub % owned, 0, keepdims=False)
    start_other = lax.ppermute(start, "core", swap)
    start = jnp.where(lax.axis_index("core") == sub // owned, start, start_other).T
    buffer, place = pack(cell_ids.reshape(1, -1), rows)
    received, start = lax.optimization_barrier((exchange(buffer), start))
    moments = moments_of(received)
    if groups > 1:
        moments = lax.psum(moments, "group")
    moments_other = lax.ppermute(moments, "core", swap)
    amount = received.shape[0]
    terms = jax.ShapeDtypeStruct((2 * WIDE, width), BF16)
    rotated, *state = stage(
        first_kernel,
        (moments, moments_other, start),
        received,
        [
            jax.ShapeDtypeStruct((amount, WIDE), BF16),
            jax.ShapeDtypeStruct((2 * width, width), BF16),
            jax.ShapeDtypeStruct((8, width), F32),
            terms, terms, terms, terms,
        ],
        2,
        80,
        "waves_0_to_2",
    )
    returned = exchange(rotated)
    (rotated_rest,) = stage(
        last_kernel,
        state,
        received,
        [jax.ShapeDtypeStruct((amount, width - WIDE), BF16)],
        3,
        50,
        "waves_3_to_4",
    )
    ready = unpack(place, returned)
    return unpack(place, exchange(rotated_rest), ready)


def solution(mesh):
    planes = mesh.shape["bucket"] // 2
    subs = CELLS // planes
    groups = mesh.shape["replica"] // subs
    owned = CELLS // mesh.shape["bucket"]
    fine = Mesh(mesh.devices.reshape(planes, 2, groups, subs), ("z", "core", "group", "sub"))
    row_split = P(("z", "core", "group", "sub"), None)
    return jax.shard_map(
        functools.partial(body, owned, groups),
        mesh=fine,
        in_specs=(row_split, row_split, P(("z", "core"), None, None)),
        out_specs=row_split,
        check_vma=False,
    )
```

```python
import functools
import itertools
import jax
import jax.numpy as jnp
from jax import lax
from jax.experimental import pallas as pl
from jax.experimental.pallas import tpu as pltpu
from jax.sharding import Mesh, PartitionSpec as P

CELLS = 16
ITERS_NS = 3
CAP = 128
BLK = 128
SUB = 16
WIDE = 256
PAD_MARK = 128.0
F32 = jnp.float32
BF16 = jnp.bfloat16
NT = (((1,), (1,)), ((), ()))
VMEM_LIMIT = 56 * 1024 * 1024


def split(value):
    high = value.astype(BF16)
    return high, (value - high.astype(F32)).astype(BF16)


def dot(left, right):
    return jnp.dot(left, right, preferred_element_type=F32)


def dot_nt(left, right):
    return lax.dot_general(left, right, NT, preferred_element_type=F32)


def product(left, right, multiply=dot):
    high, low = left
    size = high.shape[0]
    both = multiply(jnp.concatenate([high, low], axis=0), right[0])
    return both[:size, :] + (both[size:, :] + multiply(high, right[1]))


def inverse_factors(squares, beside):
    steps = BLK // SUB
    chains = range(len(squares))
    lane = lax.broadcasted_iota(jnp.int32, (SUB, BLK), 1)
    line = lax.broadcasted_iota(jnp.int32, (SUB, BLK), 0)
    parts = [[square[SUB * b : SUB * (b + 1), :] for b in range(steps)] for square in squares]
    units = [[(lane == line + SUB * b).astype(F32) for b in range(steps)] for _ in chains]
    done = [[] for _ in chains]

    def begin(n, b):
        row, carry = parts[n][b], units[n][b]
        first = SUB * b
        column = [
            jnp.broadcast_to(row[:, first + k : first + k + 1], (SUB, BLK)) for k in range(SUB)
        ]
        zeros = jnp.zeros((SUB, BLK), F32)
        return dict(column=column, row=row, carry=carry, forward=carry, pivots=zeros)

    def advance(state, k):
        q = k + 1
        column = state["column"]
        one, two = column[k], column[q]
        head, side = one[k : k + 1, :], one[q : q + 1, :]
        cross, tail = two[k : k + 1, :], two[q : q + 1, :]
        det = head * tail - cross * side
        inverse = 1.0 / det
        pair = (line == k) | (line == q)
        upper, lower = line == k, line == q
        ratio_one = jnp.where(upper, -tail, jnp.where(lower, side, one * tail - two * side)) * inverse
        ratio_two = jnp.where(upper, cross, jnp.where(lower, -head, two * head - one * cross)) * inverse

        def combined(value, left, right):
            return left * value[k : k + 1, :] + right * value[q : q + 1, :]

        def clear(value):
            return jnp.where(pair, 0.0, value) - combined(value, ratio_one, ratio_two)

        for j in range(k + 2, SUB):
            column[j] = clear(column[j])
        state["row"] = clear(state["row"])
        state["carry"] = clear(state["carry"])
        single = 1.0 / head
        low_one = jnp.where(line > q, ratio_one, jnp.where(lower, side * single, 0.0))
        low_two = jnp.where(line > q, ratio_two, 0.0)
        state["forward"] = state["forward"] - combined(state["forward"], low_one, low_two)
        state["pivots"] = jnp.where(upper, head, jnp.where(lower, det * single, state["pivots"]))

    def finish(n, b, state):
        done[n].append(state["forward"] * lax.rsqrt(state["pivots"]))
        if b + 1 == steps:
            return
        part, unit = parts[n], units[n]
        rest = jnp.concatenate(part[b + 1 :], axis=0)
        place = (lax.broadcasted_iota(jnp.int32, rest.shape, 1) - SUB * b) % BLK // SUB
        high = rest.astype(BF16).astype(F32)
        low = rest - high
        terms = jnp.where(place == 0, high, 0.0)
        terms = jnp.where(place == 1, pltpu.roll(low, SUB, 1), terms)
        terms = jnp.where(place == 2, pltpu.roll(high, 2 * SUB, 1), terms).astype(BF16)
        both = jnp.concatenate([state["row"], state["carry"]], axis=1)
        both_high, both_low = split(both)
        filled = [jnp.zeros((SUB, 2 * BLK), BF16)] * steps
        filled[b] = both_high
        filled[(b + 1) % steps] = both_high
        filled[(b + 2) % steps] = both_low
        update = dot(terms, jnp.concatenate(filled, axis=0))
        for i in range(b + 1, steps):
            at = SUB * (i - b - 1)
            part[i] = part[i] - update[at : at + SUB, :BLK]
            unit[i] = unit[i] - update[at : at + SUB, BLK:]

    for b in range(steps):
        states = [begin(n, b) for n in chains]
        for k in range(0, SUB, 2):
            for state in states:
                advance(state, k)
            beside()
        for n in chains:
            finish(n, b, states[n])
    return [jnp.concatenate(pieces, axis=0) for pieces in done]


def inverse_factors_wide(squares, beside):
    firsts = inverse_factors([square[:BLK, :BLK] for square in squares], beside)
    terms = [split(first) for first in firsts]
    factors = [
        split(product(split(square[BLK:, :BLK]), term, dot_nt))
        for square, term in zip(squares, terms)
    ]
    seconds = inverse_factors(
        [
            square[BLK:, BLK:] - product(factor, factor, dot_nt)
            for square, factor in zip(squares, factors)
        ],
        beside,
    )
    results = []
    for first, term, factor, second in zip(firsts, terms, factors, seconds):
        corner = product(split(second), split(product(factor, term)))
        upper = jnp.concatenate([first, jnp.zeros((BLK, BLK), F32)], axis=1)
        results.append(
            jnp.concatenate([upper, jnp.concatenate([-corner, second], axis=1)], axis=0)
        )
    return results


FIRST, SECOND = slice(0, WIDE), slice(WIDE, 2 * WIDE)


def terms_of(ref):
    return ref[FIRST, :], ref[SECOND, :]


def project(image, before_ref, exact):
    before = terms_of(before_ref)
    if exact:
        return image - product(split(product(split(image), before, dot_nt)), before)
    along = dot_nt(image.astype(BF16), before[0]).astype(BF16)
    return image - (dot(along, before[0]) + dot(along, before[1]))


def wave(cov_ref, tasks, beside=(), pieces=0):
    images, grams, others = [], [], [beside]
    for image_ref, before_refs, _, exact in tasks:
        image = image_ref[...]
        for before_ref in before_refs:
            image = project(image, before_ref, exact)
        image_terms = split(image)
        images.append(image_terms)
        grams.append(product(image_terms, image_terms, dot_nt))
        if not exact:
            others.insert(0, image_pieces(cov_ref, image_terms, image_ref))
            pieces += 6
    other = itertools.chain(*others)
    ticks = itertools.count()
    stride = max(1, BLK // max(1, pieces))

    def piece():
        if next(ticks) % stride == 0:
            next(other, None)

    inverses = inverse_factors_wide(grams, piece)
    for _ in other:
        pass
    for inverse, image_terms, (image_ref, _, target_ref, exact) in zip(inverses, images, tasks):
        rounded = inverse.astype(BF16)
        if not exact:
            high, low = split(image_ref[...])
            image_ref[...] = dot(rounded, high) + dot(rounded, low)
        if target_ref is None:
            continue
        if exact:
            basis = product(split(inverse), image_terms)
        else:
            basis = dot(rounded, image_terms[0]) + dot(rounded, image_terms[1])
        high, low = split(basis)
        target_ref[FIRST, :] = high
        target_ref[SECOND, :] = low


def image_pieces(cov_ref, source, image_ref):
    width = cov_ref.shape[1]
    high, low = source
    both = jnp.concatenate([high, low], axis=0)
    for n in range(width // WIDE):
        at = slice(WIDE * n, WIDE * (n + 1))
        value = dot(both, cov_ref[:width, at])
        yield
        image_ref[:, at] = value[FIRST, :] + (value[SECOND, :] + dot(high, cov_ref[width:, at]))
        yield


def project_pieces(image_ref, before_ref):
    width = image_ref.shape[1]
    along = dot_nt(image_ref[...].astype(BF16), before_ref[FIRST, :]).astype(BF16)
    yield
    for n in range(width // WIDE):
        at = slice(WIDE * n, WIDE * (n + 1))
        image_ref[:, at] = image_ref[:, at] - (
            dot(along, before_ref[FIRST, at]) + dot(along, before_ref[SECOND, at])
        )
        yield


def rotate_pieces(mean, rows_ref, rotation, out_ref, columns):
    width = mean.shape[1]
    high = mean.astype(BF16)
    left = mean - high.astype(F32)
    middle = left.astype(BF16)
    low = (left - middle.astype(F32)).astype(BF16)
    pieces = jnp.concatenate([high, middle, low, jnp.zeros((13, width), BF16)], axis=0)
    shift = jnp.sum(dot_nt(pieces, rotation), axis=0, keepdims=True)
    yield
    some = 512
    for n in range(rows_ref.shape[0] // some):
        at = slice(some * n, some * (n + 1))
        out_ref[at, columns] = (dot_nt(rows_ref[at, :], rotation) - shift).astype(BF16)
        yield


def rotate(*args):
    for _ in rotate_pieces(*args):
        pass


def first_kernel(
    moments_ref, moments_other_ref, start_ref, rows_hbm_ref,
    out_ref, cov_ref, mean_ref, q30_ref, q21_ref, image_1_ref, image_2_ref,
    rows_ref, q10_ref, q11_ref, q20_ref, image_0_ref, sem,
):
    copy = pltpu.make_async_copy(rows_hbm_ref, rows_ref, sem)
    copy.start()
    width = cov_ref.shape[1]
    tail = moments_ref[width : width + 8, :] + moments_other_ref[width : width + 8, :]
    divisor = jnp.maximum(tail[1:2, :], 1.0)
    mean = tail[0:1, :] / divisor
    mean_rows = jnp.broadcast_to(mean, (BLK, width))
    for i in range(width // BLK):
        at = slice(BLK * i, BLK * (i + 1))
        mean_column = jnp.broadcast_to(mean_rows[:, at].T[:, :1], (BLK, width))
        square = moments_ref[at, :] + moments_other_ref[at, :]
        high, low = split(square / divisor - mean_column * mean)
        cov_ref[BLK * i : BLK * (i + 1), :] = high
        cov_ref[width + BLK * i : width + BLK * (i + 1), :] = low
    mean_ref[...] = jnp.broadcast_to(mean, mean_ref.shape)

    def start(i):
        return split(start_ref[WIDE * i : WIDE * (i + 1), :])

    for _ in image_pieces(cov_ref, start(0), image_0_ref):
        pass
    wave(
        cov_ref,
        [(image_0_ref, [], q10_ref, False)],
        itertools.chain(
            image_pieces(cov_ref, start(1), image_1_ref),
            image_pieces(cov_ref, start(2), image_2_ref),
        ),
        12,
    )
    wave(
        cov_ref,
        [(image_0_ref, [], q20_ref, False), (image_1_ref, [q10_ref], q11_ref, False)],
        project_pieces(image_2_ref, q10_ref),
        4,
    )
    wave(
        cov_ref,
        [
            (image_0_ref, [], q30_ref, True),
            (image_1_ref, [q20_ref], q21_ref, False),
            (image_2_ref, [q11_ref], None, False),
        ],
        project_pieces(image_2_ref, q20_ref),
        4,
    )
    copy.wait()
    rotate(mean, rows_ref, q30_ref[FIRST, :], out_ref, FIRST)


def last_kernel(
    cov_ref, mean_ref, q30_ref, q21_ref, image_1_ref, image_in_ref, rows_hbm_ref,
    out_ref, rows_ref, q31_ref, q32_ref, image_2_ref, sem,
):
    copy = pltpu.make_async_copy(rows_hbm_ref, rows_ref, sem)
    copy.start()
    mean = mean_ref[0:1, :]
    image_2_ref[...] = image_in_ref[...]
    wave(
        cov_ref,
        [(image_1_ref, [q30_ref], q31_ref, True), (image_2_ref, [q21_ref], None, False)],
    )
    copy.wait()
    wave(
        cov_ref,
        [(image_2_ref, [q30_ref, q31_ref], q32_ref, True)],
        rotate_pieces(mean, rows_ref, q31_ref[FIRST, :], out_ref, FIRST),
        5,
    )
    rotate(mean, rows_ref, q32_ref[FIRST, :], out_ref, SECOND)


def in_vmem(amount):
    return [pl.BlockSpec(memory_space=pltpu.VMEM)] * amount


def stage(kernel, inputs, rows, outputs, kept, flops, name):
    amount, width = rows.shape
    return pl.pallas_call(
        kernel,
        out_shape=outputs,
        in_specs=in_vmem(len(inputs)) + [pl.BlockSpec(memory_space=pl.ANY)],
        out_specs=in_vmem(len(outputs)),
        scratch_shapes=[pltpu.VMEM((amount, width), BF16)]
        + kept
        + [pltpu.SemaphoreType.DMA(())],
        compiler_params=pltpu.CompilerParams(vmem_limit_bytes=VMEM_LIMIT),
        cost_estimate=pl.CostEstimate(
            flops=flops * width**3, bytes_accessed=20 * width * width, transcendentals=0
        ),
        name=name,
    )(*inputs, rows)


def moments_kernel(rows_ref, out_ref, kept_ref):
    amount, width = rows_ref.shape
    step = 256
    total = jnp.zeros((8, width), F32)
    count = jnp.zeros((8, 1), F32)
    for i in range(amount // step):
        at = slice(step * i, step * (i + 1))
        piece = rows_ref[at, :].astype(F32)
        valid = piece[:, :1] < PAD_MARK
        piece = jnp.where(valid, piece, 0.0)
        kept_ref[at, :] = piece.astype(BF16)
        total = total + jnp.sum(piece.reshape(step // 8, 8, width), axis=0)
        count = count + jnp.sum(valid.astype(F32).reshape(step // 8, 8, 1), axis=0)
    for n in range(width // 256):
        at = slice(256 * n, 256 * (n + 1))
        out_ref[at, :] = lax.dot_general(
            kept_ref[:, at], kept_ref[...], (((0,), (0,)), ((), ())), preferred_element_type=F32
        )
    line = lax.broadcasted_iota(jnp.int32, (8, width), 0)
    total = jnp.sum(total, axis=0, keepdims=True)
    count = jnp.sum(count, axis=0, keepdims=True)
    out_ref[width : width + 8, :] = jnp.where(line == 0, total, jnp.where(line == 1, count, 0.0))


def moments_of(rows):
    amount, width = rows.shape
    return pl.pallas_call(
        moments_kernel,
        out_shape=jax.ShapeDtypeStruct((width + 8, width), F32),
        in_specs=in_vmem(1),
        out_specs=pl.BlockSpec(memory_space=pltpu.VMEM),
        scratch_shapes=[pltpu.VMEM((amount, width), BF16)],
        compiler_params=pltpu.CompilerParams(vmem_limit_bytes=VMEM_LIMIT),
        name="moments",
    )(rows)


def pack_kernel(ids_ref, rows_ref, buffer_ref, place_ref):
    amount = ids_ref.shape[1]
    cell = lax.broadcasted_iota(jnp.int32, (CELLS, amount), 0)
    named = ids_ref[...] == cell
    upto = lax.broadcasted_iota(jnp.int32, (BLK, BLK), 0) <= lax.broadcasted_iota(
        jnp.int32, (BLK, BLK), 1
    )
    upto = upto.astype(BF16)
    onehot = named.astype(BF16)
    before = jnp.zeros((CELLS, 1), F32)
    goals = []
    for i in range(amount // BLK):
        at = slice(BLK * i, BLK * (i + 1))
        running = dot(onehot[:, at], upto) + before
        before = running[:, BLK - 1 :]
        goal = running - 1.0 + CAP * cell[:, at].astype(F32)
        goals.append(jnp.sum(jnp.where(named[:, at], goal, 0.0), axis=0, keepdims=True))
    goal = jnp.concatenate(goals, axis=1)
    for i in range(amount // BLK):
        at = slice(BLK * i, BLK * (i + 1))
        place_ref[at, :] = jnp.broadcast_to(goals[i], (BLK, BLK)).T
    group = 4
    slot = lax.broadcasted_iota(jnp.int32, (group * CAP, amount), 0).astype(F32)
    within = lax.broadcasted_iota(jnp.int32, (CAP, rows_ref.shape[1]), 0).astype(F32)
    for c in range(0, CELLS, group):
        hit = jnp.where(goal - float(CAP * c) == slot, 1.0, 0.0).astype(BF16)
        moved = dot(hit, rows_ref[...])
        for k in range(group):
            used = within < before[c + k : c + k + 1, :]
            part = jnp.where(used, moved[CAP * k : CAP * (k + 1), :], PAD_MARK)
            buffer_ref[c + k] = part.astype(BF16)


def unpack_kernel(place_ref, slots_ref, *refs):
    out_ref = refs[-1]
    amount, width = slots_ref.shape
    ahead = out_ref.shape[1] - width
    step = 256
    lane = lax.broadcasted_iota(jnp.int32, (step, amount), 1).astype(F32)
    for i in range(out_ref.shape[0] // step):
        at = slice(step * i, step * (i + 1))
        goal = jnp.broadcast_to(place_ref[at, :1], (step, amount))
        onehot = jnp.where(goal == lane, 1.0, 0.0).astype(BF16)
        out_ref[at, ahead:] = dot(onehot, slots_ref[...]).astype(BF16)
    first = 0
    for ready_ref in refs[:-1]:
        out_ref[:, first : first + ready_ref.shape[1]] = ready_ref[...]
        first += ready_ref.shape[1]


def pack(ids, rows):
    amount, width = rows.shape
    return pl.pallas_call(
        pack_kernel,
        out_shape=(
            jax.ShapeDtypeStruct((CELLS, CAP, width), BF16),
            jax.ShapeDtypeStruct((amount, BLK), F32),
        ),
        in_specs=in_vmem(2),
        out_specs=in_vmem(2),
        compiler_params=pltpu.CompilerParams(vmem_limit_bytes=VMEM_LIMIT),
        name="pack",
    )(ids, rows)


def unpack(place, slots, *ahead):
    width = slots.shape[1] + sum(piece.shape[1] for piece in ahead)
    return pl.pallas_call(
        unpack_kernel,
        out_shape=jax.ShapeDtypeStruct((place.shape[0], width), BF16),
        in_specs=in_vmem(2 + len(ahead)),
        out_specs=pl.BlockSpec(memory_space=pltpu.VMEM),
        compiler_params=pltpu.CompilerParams(vmem_limit_bytes=VMEM_LIMIT),
        cost_estimate=pl.CostEstimate(
            flops=2 * place.shape[0] * slots.size, bytes_accessed=4 * slots.size, transcendentals=0
        ),
        name="unpack",
    )(place, slots, *ahead)


def exchange(slots):
    width = slots.shape[-1]
    blocks = slots.reshape(CELLS, CAP, width)
    blocks = lax.all_to_all(blocks, ("z", "sub"), split_axis=0, concat_axis=0, tiled=True)
    return blocks.reshape(CELLS * CAP, width)


def body(owned, groups, rows, cell_ids, start_basis):
    width = rows.shape[1]
    swap = [(0, 1), (1, 0)]
    sub = lax.axis_index("sub")
    start = lax.dynamic_index_in_dim(start_basis, sub % owned, 0, keepdims=False)
    start_other = lax.ppermute(start, "core", swap)
    start = jnp.where(lax.axis_index("core") == sub // owned, start, start_other).T
    buffer, place = pack(cell_ids.reshape(1, -1), rows)
    received, start = lax.optimization_barrier((exchange(buffer), start))
    moments = moments_of(received)
    if groups > 1:
        moments = lax.psum(moments, "group")
    moments_other = lax.ppermute(moments, "core", swap)
    amount = received.shape[0]
    terms = jax.ShapeDtypeStruct((2 * WIDE, width), BF16)
    block = jax.ShapeDtypeStruct((WIDE, width), F32)
    basis, image = pltpu.VMEM((2 * WIDE, width), BF16), pltpu.VMEM((WIDE, width), F32)
    rotated, *state = stage(
        first_kernel,
        (moments, moments_other, start),
        received,
        [
            jax.ShapeDtypeStruct((amount, WIDE), BF16),
            jax.ShapeDtypeStruct((2 * width, width), BF16),
            jax.ShapeDtypeStruct((8, width), F32),
            terms, terms, block, block,
        ],
        [basis, basis, basis, image],
        80,
        "waves_0_to_2",
    )
    returned = exchange(rotated)
    (rotated_rest,) = stage(
        last_kernel,
        state,
        received,
        [jax.ShapeDtypeStruct((amount, width - WIDE), BF16)],
        [basis, basis, image],
        50,
        "waves_3_to_4",
    )
    ready = unpack(place, returned)
    return unpack(place, exchange(rotated_rest), ready)


def solution(mesh):
    planes = mesh.shape["bucket"] // 2
    subs = CELLS // planes
    groups = mesh.shape["replica"] // subs
    owned = CELLS // mesh.shape["bucket"]
    fine = Mesh(mesh.devices.reshape(planes, 2, groups, subs), ("z", "core", "group", "sub"))
    row_split = P(("z", "core", "group", "sub"), None)
    return jax.shard_map(
        functools.partial(body, owned, groups),
        mesh=fine,
        in_specs=(row_split, row_split, P(("z", "core"), None, None)),
        out_specs=row_split,
        check_vma=False,
    )
```
